256 devices in a mesh: expert: 32 (over z, x), tensor: 8 (over y, core).
Axes of the slice: x: 4, y: 4, z: 8, core: 2. Of those that a mesh axis runs over, the one named last changes fastest.
Arguments:
- tokens: bfloat16 [2048, 8192], P('expert', 'tensor'), may hold values from -6 to 6
- frozen_gate_weight: bfloat16 [8192, 28672], P('tensor', 'expert'), may hold values from -0.0625 to 0.0625
- frozen_up_weight: bfloat16 [8192, 28672], P('tensor', 'expert'), may hold values from -0.0625 to 0.0625
- frozen_down_weight: bfloat16 [28672, 8192], P('expert', 'tensor'), may hold values from -0.03125 to 0.03125
- adapter_down_weight: bfloat16 [128, 8192, 128], P('expert', 'tensor'), may hold values from -0.0625 to 0.0625
- adapter_up_weight: bfloat16 [128, 128, 8192], P('expert', None, 'tensor'), may hold values from -0.0625 to 0.0625
- routes: int32 [2048, 2], P('expert'), may hold values from 0 to 127, all different within a row; in each aligned block of 64 rows (0 to 63, 64 to 127, ...) at most 2 rows name the same one
- route_gate_weights: float32 [2048, 2], P('expert'), may hold values from 0.1 to 1
- output_gradient: bfloat16 [2048, 8192], P('expert', 'tensor'), may hold values from -6 to 6
Outputs:
- ffn_out: bfloat16 [2048, 8192], P('expert', 'tensor')
- grad_down: bfloat16 [128, 8192, 128], P('expert', 'tensor')
- grad_up: bfloat16 [128, 128, 8192], P('expert', None, 'tensor')
The draws below stay inside these ranges and needn't reach their ends.
Inputs may be any that keep to these rules, and one draw needn't show every extreme that they name: `routes`: the two experts of a token differ. Among the 64 rows of one index of expert no expert is named more than 2 times, and in some such rows one expert is named exactly 2 times.
All inputs are finite; a program needn't handle non-finite values.
Results may differ from the reference program's by a relative error of at most 0.025.
Values may be sent and summed in bfloat16 or wider, within the bound.
No kernel may reach another device: no remote copies, remote signals or barrier semaphores. Data moves between devices by JAX's collectives and lax.ppermute only.
A program may use at most 64 MiB of HBM per device.

```python
import math
import jax
import jax.numpy as jnp
import numpy as np
from jax import lax

MODEL_WIDTH = 8192
FF = 28672
ADAPTER_RANK = 128
TOK_DEV = 64
EXPERT_COUNT = 128
MOST = 2
TOKENS = 2048
N_EXPERT = 32
N_TENSOR = 8


def steps_of(key, shape, split, low, top_value):
    def one(dim, parts):
        heights = jax.random.uniform(jax.random.fold_in(jax.random.fold_in(key, 6), dim), (parts,), jnp.float32, low / len(split), top_value / len(split))
        return jnp.repeat(jnp.exp(heights), shape[dim] // parts).reshape((-1,) + (1,) * (len(shape) - dim - 1))

    level = one(*split[0])
    for cut in split[1:]:
        level = level * one(*cut)
    return level


def deal_out(stream_key, own, number, rows, amount, top, bound, skew):
    sequence = jax.random.permutation(stream_key, amount)
    crowded, common = portions_of(amount, rows * top, bound, skew, True), portions_of(amount, rows * top, bound, skew, False)
    places = jnp.arange(amount)

    def named(sizes, rotation):
        used = int((sizes > 0).sum())
        fixed = max(1, used // 4)
        moved = fixed + (places - fixed + rotation * (used - fixed)) % max(1, amount - fixed)
        return jnp.zeros((amount,), jnp.int32).at[sequence[jnp.where(places < fixed, places, moved)]].set(jnp.asarray(sizes, jnp.int32))

    sizes = jnp.where(number % 4 == 0, named(crowded, number // 4), named(common, number - number // 4 - 1))
    mixed = jax.random.permutation(jax.random.fold_in(own, 3), amount)
    donor, receiver = mixed[0:amount // 2 * 2:2], mixed[1:amount // 2 * 2:2]
    slack = jnp.minimum(sizes[donor] - 1, bound - sizes[receiver]) // 2
    slack = jnp.where((donor == sequence[0]) | (receiver == sequence[0]) | (sizes[receiver] == 0), 0, jnp.maximum(slack, 0))
    moved = jax.random.randint(jax.random.fold_in(own, 4), (amount // 2,), 0, 1 << 20) % (slack + 1)
    sizes = sizes.at[donor].add(-moved).at[receiver].add(moved)
    labels = jnp.searchsorted(jnp.cumsum(sizes), jnp.arange(rows * top), side="right").astype(jnp.int32)
    grid = labels.reshape(top, rows).T
    grid = grid[jax.random.permutation(jax.random.fold_in(own, 1), rows)]
    rotation = jax.random.randint(jax.random.fold_in(own, 2), (rows, 1), 0, top)
    return jnp.take_along_axis(grid, (jnp.arange(top)[None, :] + rotation) % top, axis=1)


def portions_of(amount, total, most, skew, full):
    loads = [(1 << 20) // math.isqrt(standing ** skew) + 1 for standing in range(1, amount + 1)]
    largest = most if full else min(most, max(-(-total // amount), total * loads[0] // sum(loads)))
    least = 1 if total - largest >= amount - 1 else 0
    counts, rest = [largest] + [least] * (amount - 1), total - largest - least * (amount - 1)
    while rest > 0:
        free = [i for i in range(1, amount) if counts[i] < largest] or [i for i in range(1, amount) if counts[i] < most]
        whole, left = sum([loads[i] for i in free]), rest
        for i in free:
            extra = min(most - counts[i], max(1, left * loads[i] // whole), rest)
            counts[i] = counts[i] + extra
            rest = rest - extra
    return np.array(counts)


def scatter_about(rng, dims, scale, most, split=(), kind=jnp.bfloat16):
    factor_of = steps_of(rng, dims, split, -0.22, 0.18) if split else 1.0
    values = jax.random.normal(rng, dims, jnp.float32) * scale * factor_of
    return jnp.minimum(jnp.maximum(values, -most), most).astype(kind)


def setup_inputs(seed: int = 0) -> dict:
    splits = jax.random.split(jax.random.key(seed), 10)
    tokens = scatter_about(splits[0], (TOKENS, MODEL_WIDTH), 1.0, 6.0, ((0, 32), (1, 8)))
    frozen_gate_weight = scatter_about(splits[1], (MODEL_WIDTH, FF), MODEL_WIDTH ** -0.5, 0.0625, ((0, 8), (1, 32)))
    frozen_up_weight = scatter_about(splits[2], (MODEL_WIDTH, FF), MODEL_WIDTH ** -0.5, 0.0625, ((0, 8), (1, 32)))
    frozen_down_weight = scatter_about(splits[3], (FF, MODEL_WIDTH), FF ** -0.5, 0.03125, ((0, 32), (1, 8)))
    adapter_down_weight = scatter_about(splits[4], (EXPERT_COUNT, MODEL_WIDTH, ADAPTER_RANK), MODEL_WIDTH ** -0.5, 0.0625, ((0, 32), (1, 8)))
    adapter_up_weight = scatter_about(splits[5], (EXPERT_COUNT, ADAPTER_RANK, MODEL_WIDTH), MODEL_WIDTH ** -0.5, 0.0625, ((0, 32), (2, 8)))
    routes_keys = jax.random.split(jax.random.fold_in(splits[6], 1), TOKENS // TOK_DEV)
    routes_turns = jax.random.permutation(jax.random.fold_in(splits[6], 3), TOKENS // TOK_DEV)
    routes = jax.vmap(lambda own, number: deal_out(jax.random.fold_in(splits[6], 2), own, number, TOK_DEV, EXPERT_COUNT, 2, MOST, 2))(routes_keys, routes_turns).reshape((TOKENS, 2))
    route_gate_weights = jnp.clip(0.1 + 0.9 * jax.random.uniform(splits[7], (TOKENS, 2), jnp.float32) ** steps_of(splits[7], (TOKENS, 2), ((0, 32),), -0.2, 0.2), 0.1, 1.0)
    output_gradient = scatter_about(splits[8], (TOKENS, MODEL_WIDTH), 1.0, 6.0, ((0, 32), (1, 8)))
    return dict(tokens=tokens, frozen_gate_weight=frozen_gate_weight, frozen_up_weight=frozen_up_weight, frozen_down_weight=frozen_down_weight, adapter_down_weight=adapter_down_weight, adapter_up_weight=adapter_up_weight, routes=routes, route_gate_weights=route_gate_weights, output_gradient=output_gradient)


def rounded(values):
    return lax.optimization_barrier(values.astype(jnp.bfloat16)).astype(jnp.float32)


def reference(tokens, frozen_gate_weight, frozen_up_weight, frozen_down_weight, adapter_down_weight, adapter_up_weight, routes, route_gate_weights, output_gradient):
    width_part = MODEL_WIDTH // N_TENSOR
    hidden_part = FF // N_EXPERT

    def gate_block(index, carry):
        first_col = (jnp.asarray(index) * width_part).astype(jnp.int32)
        block_rows = lax.dynamic_slice_in_dim(tokens, first_col, width_part, 1)
        gate_rows = lax.dynamic_slice_in_dim(frozen_gate_weight, first_col, width_part, 0)
        up_rows = lax.dynamic_slice_in_dim(frozen_up_weight, first_col, width_part, 0)
        gate_term = rounded(jnp.dot(block_rows, gate_rows, preferred_element_type=jnp.float32))
        up_term = rounded(jnp.dot(block_rows, up_rows, preferred_element_type=jnp.float32))
        return (carry[0] + gate_term, carry[1] + up_term)

    zero_hidden = jnp.zeros((TOKENS, FF), jnp.float32)
    gate_sum, up_sum = lax.fori_loop(0, N_TENSOR, gate_block, (zero_hidden, zero_hidden))
    hidden = (jax.nn.silu(gate_sum) * up_sum).astype(jnp.bfloat16)

    def down_block(index, carry):
        first_col = (jnp.asarray(index) * hidden_part).astype(jnp.int32)
        block_cols = lax.dynamic_slice_in_dim(hidden, first_col, hidden_part, 1)
        down_rows = lax.dynamic_slice_in_dim(frozen_down_weight, first_col, hidden_part, 0)
        return carry + rounded(jnp.dot(block_cols, down_rows, preferred_element_type=jnp.float32))

    base_out = lax.fori_loop(0, N_EXPERT, down_block, jnp.zeros((TOKENS, MODEL_WIDTH), jnp.float32))

    route_ids = routes.reshape(-1)
    gate_flat = route_gate_weights.reshape(-1)
    capacity = MOST * N_EXPERT

    def per_expert(adapter_sum, expert_slot):
        hits = route_ids == expert_slot
        total_hits = jnp.sum(hits.astype(jnp.int32))
        picks = jnp.nonzero(hits, size=capacity, fill_value=0)[0].astype(jnp.int32)
        valid = jnp.arange(capacity, dtype=jnp.int32) < total_hits
        token_index = (picks // 2).astype(jnp.int32)
        weights = jnp.where(valid, gate_flat[picks], jnp.float32(0.0))
        inputs = jnp.where(valid[:, None], tokens[token_index], jnp.zeros((), jnp.bfloat16))
        down_matrix = adapter_down_weight[expert_slot]
        up_matrix = adapter_up_weight[expert_slot]
        rank_activations = jnp.dot(inputs, down_matrix, preferred_element_type=jnp.float32).astype(jnp.bfloat16)
        expert_out = jnp.dot(rank_activations, up_matrix, preferred_element_type=jnp.float32).astype(jnp.bfloat16)
        adapter_sum = adapter_sum.at[token_index].add(weights[:, None] * expert_out.astype(jnp.float32))
        scaled = (weights[:, None] * output_gradient[token_index].astype(jnp.float32)).astype(jnp.bfloat16)
        grad_b = jnp.dot(rank_activations.T, scaled, preferred_element_type=jnp.float32).astype(jnp.bfloat16)
        back_low = jnp.dot(scaled, up_matrix.T, preferred_element_type=jnp.float32).astype(jnp.bfloat16)
        grad_a = jnp.dot(inputs.T, back_low, preferred_element_type=jnp.float32).astype(jnp.bfloat16)
        return adapter_sum, (grad_a, grad_b)

    adapter_sum, (grad_down, grad_up) = lax.scan(per_expert, jnp.zeros((TOKENS, MODEL_WIDTH), jnp.float32), jnp.arange(EXPERT_COUNT, dtype=jnp.int32))
    ffn_out = (base_out + adapter_sum).astype(jnp.bfloat16)
    return ffn_out, grad_down, grad_up
```

```python
import jax
import jax.numpy as jnp
from jax import lax
from jax.sharding import Mesh, PartitionSpec as P

BF = jnp.bfloat16
F32 = jnp.float32
NZ, NX, NY, NC = 8, 4, 4, 2


def tie(value, *after):
    return lax.optimization_barrier((value,) + after)[0]


def from_peer(value, axis, offset):
    n = lax.axis_size(axis)
    return lax.ppermute(value, axis, [(i, (i - offset) % n) for i in range(n)])


def direct_gather(value, axis):
    n = lax.axis_size(axis)
    return [value] + [from_peer(value, axis, d) for d in range(1, n)]


def ring_gather(value, axis):
    n = lax.axis_size(axis)
    held = [None] * n
    held[0] = up = down = value
    for step in range(1, n // 2 + 1):
        up = from_peer(up, axis, 1)
        held[step] = up
        if step <= (n - 1) // 2:
            down = from_peer(down, axis, -1)
            held[n - step] = down
    return held


def plus(a, b):
    return (a.astype(F32) + b.astype(F32)).astype(BF)


def ring_reduce(blocks, axis):
    n = lax.axis_size(axis)
    sides = []
    for sign, far in ((1, n // 2), (-1, (n - 1) // 2)):
        moving = blocks[(sign * far) % n]
        for d in range(far - 1, -1, -1):
            moving = from_peer(moving, axis, -sign)
            if d:
                moving = plus(moving, blocks[(sign * d) % n])
        sides.append(moving)
    return blocks[0].astype(F32) + sides[0].astype(F32) + sides[1].astype(F32)


def gather_tokens(tokens):
    half = tokens.shape[0] // 2
    first, second = tokens[:half], tokens[half:]
    first = jnp.concatenate(direct_gather(first, "x"), 0)
    second = jnp.concatenate(direct_gather(second, "z"), 0)
    return ring_gather(first, "z") + direct_gather(second, "x")


def reduce_rows(out):
    half = out.shape[0] // 2
    step = half // NZ
    first = [out[d * step : (d + 1) * step] for d in range(NZ)]
    step = half // NX
    second = [out[half + d * step : half + (d + 1) * step] for d in range(NX)]
    first = ring_reduce(first, "z").astype(BF)
    second = ring_reduce(second, "x").astype(BF)
    step = first.shape[0] // NX
    first = ring_reduce([first[d * step : (d + 1) * step] for d in range(NX)], "x")
    step = second.shape[0] // NZ
    second = ring_reduce([second[d * step : (d + 1) * step] for d in range(NZ)], "z")
    return jnp.concatenate([first, second], 0)


def gather_hidden(hidden, buffer):
    rows = hidden.shape[0]
    y, c = lax.axis_index("y"), lax.axis_index("c")
    own = direct_gather(hidden, "y")
    for d in range(NY):
        place = (((y + d) % NY) * NC + c) * rows
        buffer = lax.dynamic_update_slice(buffer, own[d], (place, 0))
        other = from_peer(own[d], "c", 1)
        place = (((y + d) % NY) * NC + 1 - c) * rows
        buffer = lax.dynamic_update_slice(buffer, other, (place, 0))
    return buffer


def sum_over_tensor(part):
    pair = plus(part, from_peer(part, "c", 1))
    total = pair.astype(F32)
    for d in (1, 3, 2):
        total = total + from_peer(pair, "y", d).astype(F32)
    return total.astype(BF)


def per_device(
    tokens,
    frozen_gate_weight,
    frozen_up_weight,
    frozen_down_weight,
    adapter_down_weight,
    adapter_up_weight,
    routes,
    route_gate_weights,
    output_gradient,
):
    tok_count, width = tokens.shape
    hidden_width = frozen_gate_weight.shape[1]
    resident = adapter_down_weight.shape[0]
    peers = NZ * NX
    most = 2
    per_peer = resident * most
    slots = peers * per_peer
    all_rows = peers * tok_count

    with jax.named_scope("gather_tokens"):
        shard_rows = jnp.concatenate(gather_tokens(tokens), 0)
    gate_up_weight = jnp.concatenate([frozen_gate_weight, frozen_up_weight], 1)

    with jax.named_scope("routing"):
        ids = routes.reshape(-1)
        pairs = ids.shape[0]
        pair = jnp.arange(pairs, dtype=jnp.int32)
        same = (ids[:, None] == ids[None, :]) & (pair[:, None] > pair[None, :])
        target = ids * most + jnp.sum(same.astype(jnp.int32), axis=1)
        slot = jnp.arange(slots, dtype=jnp.int32)
        select = (slot[:, None] == target[None, :]).astype(BF)
        scaled = (route_gate_weights[:, :, None] * output_gradient[:, None, :].astype(F32)).astype(BF)
        scaled = scaled.reshape(pairs, width)
        weight = route_gate_weights.reshape(pairs, 1)
        high = weight.astype(BF)
        rest = weight - high.astype(F32)
        middle = rest.astype(BF)
        low_bits = (rest - middle.astype(F32)).astype(BF)
        place = (pair // 2 + 1).astype(BF).reshape(pairs, 1)
        extra = jnp.concatenate(
            [place, high, middle, low_bits, jnp.zeros((pairs, 124), BF)], 1
        )
        send = jnp.dot(select, jnp.concatenate([scaled, extra], 1), preferred_element_type=F32)
        send = send.astype(BF).reshape(peers, per_peer, width + 128)
    with jax.named_scope("exchange_gradients"):
        got = lax.all_to_all(send, ("z", "x"), split_axis=0, concat_axis=0, tiled=True)
    with jax.named_scope("slots"):
        got = got.reshape(peers, resident, most, width + 128).transpose(1, 0, 2, 3)
        got = got.reshape(resident, peers * most, width + 128)
        incoming_gradients = got[:, :, :width]
        extra = got[:, :, width : width + 4].astype(F32).reshape(resident * peers * most, 4)
        place = extra[:, 0].astype(jnp.int32) - 1
        weight = extra[:, 1] + extra[:, 2] + extra[:, 3]
        source = (jnp.arange(resident * peers * most, dtype=jnp.int32) // most) % peers
        dz = (source // NX - lax.axis_index("z")) % NZ
        dx = (source % NX - lax.axis_index("x")) % NX
        half = tok_count // 2
        row = jnp.where(
            place < half,
            (dz * NX + dx) * half + place,
            all_rows // 2 + (dx * NZ + dz) * half + place - half,
        )
        row = jnp.where(place < 0, -1, row)
        rows = jnp.arange(all_rows, dtype=jnp.int32)
        pick = (row[:, None] == rows[None, :]).astype(BF)
        put = (rows[:, None] == row[None, :]).astype(BF)

    with jax.named_scope("gate_up"):
        partial_value = jnp.dot(shard_rows, gate_up_weight, preferred_element_type=F32).astype(BF)
    with jax.named_scope("reduce_gate_up"):
        summed = lax.psum_scatter(
            partial_value, ("y", "c"), scatter_dimension=0, tiled=True
        ).astype(F32)
    with jax.named_scope("activate"):
        hidden = (jax.nn.silu(summed[:, :hidden_width]) * summed[:, hidden_width:]).astype(BF)

    with jax.named_scope("low_rank"):
        incoming_rows = jnp.dot(pick, shard_rows, preferred_element_type=F32).astype(BF)
        incoming_rows = incoming_rows.reshape(resident, peers * most, width)
        low = jnp.einsum(
            "csk,cko->cso", incoming_rows, adapter_down_weight, preferred_element_type=F32
        ).astype(BF)
        back = jnp.einsum(
            "csf,cxf->csx", incoming_gradients, adapter_up_weight, preferred_element_type=F32
        ).astype(BF)
    with jax.named_scope("sum_low_rank"):
        both = sum_over_tensor(jnp.concatenate([low, back], 0))
        low, back = both[:resident], both[resident:]
    with jax.named_scope("adapter_out"):
        expert_out = jnp.einsum(
            "csx,cxo->cso", low, adapter_up_weight, preferred_element_type=F32
        ).astype(BF)
        expert_out = expert_out.reshape(slots, width)
        weighted = (weight[:, None] * expert_out.astype(F32)).astype(BF)
    with jax.named_scope("adapter_grads"):
        grad_up = jnp.einsum(
            "csr,csd->crd", low, incoming_gradients, preferred_element_type=F32
        ).astype(BF)
        grad_down = jnp.einsum(
            "csd,csr->cdr", incoming_rows, back, preferred_element_type=F32
        ).astype(BF)

    with jax.named_scope("gather_hidden"):
        buffer = jnp.concatenate([jnp.zeros((all_rows, hidden_width), BF), put], 1)
        hidden_all = gather_hidden(hidden, buffer)
    with jax.named_scope("down"):
        down_weight = jnp.concatenate([frozen_down_weight, weighted], 0)
        out = jnp.dot(hidden_all, down_weight, preferred_element_type=F32).astype(BF)
    with jax.named_scope("reduce_rows"):
        ffn_out = reduce_rows(out).astype(BF)
    return (ffn_out, grad_down, grad_up)


def solution(mesh):
    split = Mesh(mesh.devices.reshape(NZ, NX, NY, NC), ("z", "x", "y", "c"))
    e, t = ("z", "x"), ("y", "c")
    placed = (
        P(e, t),
        P(t, e),
        P(t, e),
        P(e, t),
        P(e, t, None),
        P(e, None, t),
        P(e, None),
        P(e, None),
        P(e, t),
    )
    return jax.shard_map(
        per_device,
        mesh=split,
        in_specs=placed,
        out_specs=(P(e, t), P(e, t, None), P(e, None, t)),
        check_vma=False,
    )
```

```python
import jax
import jax.numpy as jnp
from jax import lax
from jax.sharding import Mesh, PartitionSpec as P

BF = jnp.bfloat16
F32 = jnp.float32
NZ, NX, NY, NC = 8, 4, 4, 2


def tie(value, *after):
    return lax.optimization_barrier((value,) + after)[0]


def from_peer(value, axis, offset):
    n = lax.axis_size(axis)
    return lax.ppermute(value, axis, [(i, (i - offset) % n) for i in range(n)])


def direct_gather(value, axis):
    n = lax.axis_size(axis)
    return [value] + [from_peer(value, axis, d) for d in range(1, n)]


def plus(a, b):
    return (a.astype(F32) + b.astype(F32)).astype(BF)


def ring_reduce(blocks, axis, beside):
    n = lax.axis_size(axis)
    far = {1: n // 2, -1: (n - 1) // 2}
    moving = {sign: blocks[(sign * far[sign]) % n] for sign in far}
    for d in range(n // 2 - 1, -1, -1):
        if d == 1:
            moving[1], moving[-1], beside = lax.optimization_barrier((moving[1], moving[-1], beside))
        for sign in far:
            if d < far[sign]:
                moving[sign] = from_peer(moving[sign], axis, -sign)
                if d:
                    moving[sign] = plus(moving[sign], blocks[(sign * d) % n])
    return blocks[0].astype(F32) + moving[1].astype(F32) + moving[-1].astype(F32), beside


def ring_gather(values, axis):
    n = lax.axis_size(axis)
    held = [[value] + [None] * (n - 1) for value in values]
    up, down = list(values), list(values)
    for step in range(1, n // 2 + 1):
        for i in range(len(values)):
            if step > 2:
                behind = held[1 - i][step - 2 + i]
                up[i], down[i], behind = lax.optimization_barrier((up[i], down[i], behind))
                held[1 - i][step - 2 + i] = behind
            up[i] = from_peer(up[i], axis, 1)
            held[i][step] = up[i]
            if step <= (n - 1) // 2:
                down[i] = from_peer(down[i], axis, -1)
                held[i][n - step] = down[i]
    return jnp.concatenate([block for blocks in held for block in blocks], 0)


def gather_tokens(tokens):
    blocks = direct_gather(tokens, "x")
    return ring_gather([jnp.concatenate(blocks[:2], 0), jnp.concatenate(blocks[2:], 0)], "z")


def row_of(z, x, place, rows):
    dz, dx = (z - lax.axis_index("z")) % NZ, (x - lax.axis_index("x")) % NX
    return ((dx // 2 * NZ + dz) * 2 + dx % 2) * rows + place


def in_order(out):
    return jnp.concatenate([block_rows(out, half * NZ + dz) for dz in range(NZ) for half in (0, 1)], 0)


def block_rows(out, index):
    step = out.shape[0] // (2 * NY * NC)
    device = index // 2
    place = (device // NC - lax.axis_index("y")) % NY * NC + (device % NC - lax.axis_index("c")) % NC
    return lax.dynamic_slice_in_dim(out, (place * 2 + index % 2) * step, step, 0)


def exchange(blocks, axis):
    return lax.all_to_all(blocks, axis, split_axis=0, concat_axis=0, tiled=True)


def reduce_rows(out):
    rows, width = out.shape
    cut, step = width * 5 // 8, rows // NZ
    near = out[:, cut:].reshape(NZ, NX, step // NX, width - cut)
    near = jnp.concatenate([near[:, d].reshape(-1, width - cut) for d in range(NX)], 0)
    near = direct_reduce(near, "x").astype(BF)
    far, near = ring_reduce([out[d * step : (d + 1) * step, :cut] for d in range(NZ)], "z", near)
    far = far.astype(BF)
    step = near.shape[0] // NZ
    turn = (NZ - lax.axis_index("z")) % NZ * step
    near = lax.dynamic_slice_in_dim(jnp.concatenate([near, near], 0), turn, NZ * step, 0)
    near = jnp.sum(exchange(near.reshape(NZ, step, width - cut), "z").astype(F32), 0)
    return jnp.concatenate([direct_reduce(far, "x"), near], 1)


def direct_reduce(part, axis):
    n = lax.axis_size(axis)
    step = part.shape[0] // n
    total = part[:step].astype(F32)
    for d in range(1, n):
        total = total + from_peer(part[d * step : (d + 1) * step], axis, -d).astype(F32)
    return total


def gather_hidden(hidden):
    return [jnp.concatenate([piece, from_peer(piece, "c", 1)], 0) for piece in direct_gather(hidden, "y")]


def sum_over_tensor(part):
    pair = plus(part, from_peer(part, "c", 1))
    total = pair.astype(F32)
    for d in (1, 3, 2):
        total = total + from_peer(pair, "y", d).astype(F32)
    return total.astype(BF)


def per_device(
    tokens,
    frozen_gate_weight,
    frozen_up_weight,
    frozen_down_weight,
    adapter_down_weight,
    adapter_up_weight,
    routes,
    route_gate_weights,
    output_gradient,
):
    tok_count, width = tokens.shape
    hidden_width = frozen_gate_weight.shape[1]
    resident = adapter_down_weight.shape[0]
    peers = NZ * NX
    most = 2
    per_peer = resident * most
    slots = peers * per_peer
    all_rows = peers * tok_count

    with jax.named_scope("gather_tokens"):
        shard_rows = gather_tokens(tokens)
    gate_up_weight = jnp.concatenate([frozen_gate_weight, frozen_up_weight], 1)

    with jax.named_scope("gate_up"):
        partial_value = jnp.dot(shard_rows, gate_up_weight, preferred_element_type=F32).astype(BF)
    with jax.named_scope("reduce_gate_up"):
        summed = lax.psum_scatter(
            partial_value, ("y", "c"), scatter_dimension=0, tiled=True
        ).astype(F32)
    with jax.named_scope("activate"):
        hidden = (jax.nn.silu(summed[:, :hidden_width]) * summed[:, hidden_width:]).astype(BF)

    with jax.named_scope("routing"):
        ids = routes.reshape(-1)
        pairs = ids.shape[0]
        pair = jnp.arange(pairs, dtype=jnp.int32)
        same = (ids[:, None] == ids[None, :]) & (pair[:, None] > pair[None, :])
        target = ids * most + jnp.sum(same.astype(jnp.int32), axis=1)
        slot = jnp.arange(slots, dtype=jnp.int32)
        select = (slot[:, None] == target[None, :]).astype(BF)
        scaled = (route_gate_weights[:, :, None] * output_gradient[:, None, :].astype(F32)).astype(BF)
        scaled = scaled.reshape(pairs, width)
        weight = route_gate_weights.reshape(pairs, 1)
        high = weight.astype(BF)
        rest = weight - high.astype(F32)
        middle = rest.astype(BF)
        low_bits = (rest - middle.astype(F32)).astype(BF)
        place = (pair // 2 + 1).astype(BF).reshape(pairs, 1)
        extra = jnp.concatenate(
            [place, high, middle, low_bits, jnp.zeros((pairs, 124), BF)], 1
        )
        send = jnp.dot(select, jnp.concatenate([scaled, extra], 1), preferred_element_type=F32)
        send = send.astype(BF).reshape(peers, per_peer, width + 128)
    with jax.named_scope("exchange_gradients"):
        send = tie(send, partial_value)
        got = lax.all_to_all(send, ("z", "x"), split_axis=0, concat_axis=0, tiled=True)
    with jax.named_scope("slots"):
        got = got.reshape(peers, resident, most, width + 128).transpose(1, 0, 2, 3)
        got = got.reshape(resident, peers * most, width + 128)
        incoming_gradients = got[:, :, :width]
        extra = got[:, :, width : width + 4].astype(F32).reshape(resident * peers * most, 4)
        place = extra[:, 0].astype(jnp.int32) - 1
        weight = extra[:, 1] + extra[:, 2] + extra[:, 3]
        source = (jnp.arange(resident * peers * most, dtype=jnp.int32) // most) % peers
        z, x = source // NX, source % NX
        row = row_of(z, x, place, tok_count)
        row = jnp.where(place < 0, -1, row)
        rows = jnp.arange(all_rows, dtype=jnp.int32)
        pick = (row[:, None] == rows[None, :]).astype(BF)
        block = all_rows // (NY * NC)
        device = rows // block
        device = (device // NC + lax.axis_index("y")) % NY * NC + (device + lax.axis_index("c")) % NC
        held_row = device * block + rows % block
        put = (held_row[:, None] == row[None, :]).astype(BF)

    with jax.named_scope("low_rank"):
        incoming_rows = jnp.dot(pick, shard_rows, preferred_element_type=F32)
        incoming_rows = incoming_rows.astype(BF)
        incoming_rows = incoming_rows.reshape(resident, peers * most, width)
        low = jnp.einsum(
            "csk,cko->cso", incoming_rows, adapter_down_weight, preferred_element_type=F32
        ).astype(BF)
        back = jnp.einsum(
            "csf,cxf->csx", incoming_gradients, adapter_up_weight, preferred_element_type=F32
        ).astype(BF)
    with jax.named_scope("sum_low_rank"):
        both = sum_over_tensor(jnp.concatenate([low, back], 0))
        low, back = both[:resident], both[resident:]
    with jax.named_scope("adapter_out"):
        expert_out = jnp.einsum(
            "csx,cxo->cso", low, adapter_up_weight, preferred_element_type=F32
        ).astype(BF)
        expert_out = expert_out.reshape(slots, width)
        weighted = (weight[:, None] * expert_out.astype(F32)).astype(BF)
    with jax.named_scope("adapter_grads"):
        grad_up = jnp.einsum(
            "csr,csd->crd", low, incoming_gradients, preferred_element_type=F32
        ).astype(BF)
        grad_down = jnp.einsum(
            "csd,csr->cdr", incoming_rows, back, preferred_element_type=F32
        ).astype(BF)

    with jax.named_scope("gather_hidden"):
        pieces = gather_hidden(hidden)
    with jax.named_scope("down"):
        down_weight = jnp.concatenate([frozen_down_weight, weighted], 0)
        put = put.reshape(NY, -1, slots)
        out = [
            jnp.dot(
                jnp.concatenate([piece, put[d]], 1), down_weight, preferred_element_type=F32
            ).astype(BF)
            for d, piece in enumerate(pieces)
        ]
        out = jnp.concatenate(out, 0)
        out, grad_up, grad_down = lax.optimization_barrier((out, grad_up, grad_down))
    with jax.named_scope("reduce_rows"):
        ffn_out = reduce_rows(in_order(out)).astype(BF)
    return (ffn_out, grad_down, grad_up)


def solution(mesh):
    split = Mesh(mesh.devices.reshape(NZ, NX, NY, NC), ("z", "x", "y", "c"))
    e, t = ("z", "x"), ("y", "c")
    placed = (
        P(e, t),
        P(t, e),
        P(t, e),
        P(e, t),
        P(e, t, None),
        P(e, None, t),
        P(e, None),
        P(e, None),
        P(e, t),
    )
    return jax.shard_map(
        per_device,
        mesh=split,
        in_specs=placed,
        out_specs=(P(e, t), P(e, t, None), P(e, None, t)),
        check_vma=False,
    )
```

```python
import jax
import jax.numpy as jnp
from jax import lax
from jax.sharding import Mesh, PartitionSpec as P

BF = jnp.bfloat16
F32 = jnp.float32
NZ, NX, NY, NC = 8, 4, 4, 2


def tie(value, *after):
    return lax.optimization_barrier((value,) + after)[0]


def from_peer(value, axis, offset):
    n = lax.axis_size(axis)
    return lax.ppermute(value, axis, [(i, (i - offset) % n) for i in range(n)])


def direct_gather(value, axis):
    n = lax.axis_size(axis)
    return [value] + [from_peer(value, axis, d) for d in range(1, n)]


def plus(a, b):
    return (a.astype(F32) + b.astype(F32)).astype(BF)


def ring_reduce(blocks, axis, beside):
    n = lax.axis_size(axis)
    far = {1: n // 2, -1: (n - 1) // 2}
    moving = {sign: blocks[(sign * far[sign]) % n] for sign in far}
    for d in range(n // 2 - 1, -1, -1):
        if d == 0:
            moving[1], moving[-1], beside = lax.optimization_barrier((moving[1], moving[-1], beside))
        for sign in far:
            if d < far[sign]:
                moving[sign] = from_peer(moving[sign], axis, -sign)
                if d:
                    moving[sign] = plus(moving[sign], blocks[(sign * d) % n])
    return blocks[0].astype(F32) + moving[1].astype(F32) + moving[-1].astype(F32), beside


def ring_gather(values, axis):
    n = lax.axis_size(axis)
    held = [[value] + [None] * (n - 1) for value in values]
    up, down = list(values), list(values)
    for step in range(1, n // 2 + 1):
        for i in range(len(values)):
            if step > 2:
                behind = held[1 - i][step - 2 + i]
                up[i], down[i], behind = lax.optimization_barrier((up[i], down[i], behind))
                held[1 - i][step - 2 + i] = behind
            up[i] = from_peer(up[i], axis, 1)
            held[i][step] = up[i]
            if step <= (n - 1) // 2:
                down[i] = from_peer(down[i], axis, -1)
                held[i][n - step] = down[i]
    return jnp.concatenate([block for blocks in held for block in blocks], 0)


def gather_tokens(tokens):
    blocks = direct_gather(tokens, "x")
    return ring_gather([jnp.concatenate(blocks[:2], 0), jnp.concatenate(blocks[2:], 0)], "z")


def row_of(z, x, place, rows):
    dz, dx = (z - lax.axis_index("z")) % NZ, (x - lax.axis_index("x")) % NX
    return ((dx // 2 * NZ + dz) * 2 + dx % 2) * rows + place


def in_order(out):
    return jnp.concatenate([block_rows(out, half * NZ + dz) for dz in range(NZ) for half in (0, 1)], 0)


def block_rows(out, index):
    step = out.shape[0] // (2 * NY * NC)
    device = index // 2
    place = (device // NC - lax.axis_index("y")) % NY * NC + (device % NC - lax.axis_index("c")) % NC
    return lax.dynamic_slice_in_dim(out, (place * 2 + index % 2) * step, step, 0)


def exchange(blocks, axis):
    return lax.all_to_all(blocks, axis, split_axis=0, concat_axis=0, tiled=True)


def reduce_rows(out):
    rows, width = out.shape
    cut, step = width * 5 // 8, rows // NZ
    near = out[:, cut:].reshape(NZ, NX, step // NX, width - cut)
    near = jnp.concatenate([near[:, d].reshape(-1, width - cut) for d in range(NX)], 0)
    near = direct_reduce(near, "x").astype(BF)
    block = near.shape[0] // NZ
    near = lax.dynamic_slice_in_dim(
        jnp.concatenate([near, near], 0), (NZ - lax.axis_index("z")) % NZ * block, NZ * block, 0
    )
    far, near = ring_reduce([out[d * step : (d + 1) * step, :cut] for d in range(NZ)], "z", near)
    near = exchange(near.reshape(NZ, block, width - cut), "z")
    near = jnp.sum(near.astype(F32), 0)
    far = far.astype(BF)
    return jnp.concatenate([direct_reduce(far, "x"), near], 1)


def direct_reduce(part, axis):
    n = lax.axis_size(axis)
    step = part.shape[0] // n
    total = part[:step].astype(F32)
    for d in range(1, n):
        total = total + from_peer(part[d * step : (d + 1) * step], axis, -d).astype(F32)
    return total


def gather_hidden(hidden):
    return [jnp.concatenate([piece, from_peer(piece, "c", 1)], 0) for piece in direct_gather(hidden, "y")]


def sum_over_tensor(part):
    pair = plus(part, from_peer(part, "c", 1))
    total = pair.astype(F32)
    for d in (1, 3, 2):
        total = total + from_peer(pair, "y", d).astype(F32)
    return total.astype(BF)


def per_device(
    tokens,
    frozen_gate_weight,
    frozen_up_weight,
    frozen_down_weight,
    adapter_down_weight,
    adapter_up_weight,
    routes,
    route_gate_weights,
    output_gradient,
):
    tok_count, width = tokens.shape
    hidden_width = frozen_gate_weight.shape[1]
    resident = adapter_down_weight.shape[0]
    peers = NZ * NX
    most = 2
    per_peer = resident * most
    slots = peers * per_peer
    all_rows = peers * tok_count

    with jax.named_scope("gather_tokens"):
        shard_rows = gather_tokens(tokens)
    gate_up_weight = jnp.concatenate([frozen_gate_weight, frozen_up_weight], 1)

    with jax.named_scope("gate_up"):
        partial_value = jnp.dot(shard_rows, gate_up_weight, preferred_element_type=F32).astype(BF)
    with jax.named_scope("reduce_gate_up"):
        summed = lax.psum_scatter(
            partial_value, ("y", "c"), scatter_dimension=0, tiled=True
        ).astype(F32)
    with jax.named_scope("activate"):
        hidden = (jax.nn.silu(summed[:, :hidden_width]) * summed[:, hidden_width:]).astype(BF)

    with jax.named_scope("routing"):
        ids = routes.reshape(-1)
        pairs = ids.shape[0]
        pair = jnp.arange(pairs, dtype=jnp.int32)
        same = (ids[:, None] == ids[None, :]) & (pair[:, None] > pair[None, :])
        target = ids * most + jnp.sum(same.astype(jnp.int32), axis=1)
        slot = jnp.arange(slots, dtype=jnp.int32)
        select = (slot[:, None] == target[None, :]).astype(BF)
        scaled = (route_gate_weights[:, :, None] * output_gradient[:, None, :].astype(F32)).astype(BF)
        scaled = scaled.reshape(pairs, width)
        weight = route_gate_weights.reshape(pairs, 1)
        high = weight.astype(BF)
        rest = weight - high.astype(F32)
        middle = rest.astype(BF)
        low_bits = (rest - middle.astype(F32)).astype(BF)
        place = (pair // 2 + 1).astype(BF).reshape(pairs, 1)
        extra = jnp.concatenate(
            [place, high, middle, low_bits, jnp.zeros((pairs, 124), BF)], 1
        )
        send = jnp.dot(select, jnp.concatenate([scaled, extra], 1), preferred_element_type=F32)
        send = send.astype(BF).reshape(peers, per_peer, width + 128)
    with jax.named_scope("exchange_gradients"):
        send = tie(send, partial_value)
        got = lax.all_to_all(send, ("z", "x"), split_axis=0, concat_axis=0, tiled=True)
    with jax.named_scope("slots"):
        got = got.reshape(peers, resident, most, width + 128).transpose(1, 0, 2, 3)
        got = got.reshape(resident, peers * most, width + 128)
        incoming_gradients = got[:, :, :width]
        extra = got[:, :, width : width + 4].astype(F32).reshape(resident * peers * most, 4)
        place = extra[:, 0].astype(jnp.int32) - 1
        weight = extra[:, 1] + extra[:, 2] + extra[:, 3]
        source = (jnp.arange(resident * peers * most, dtype=jnp.int32) // most) % peers
        z, x = source // NX, source % NX
        row = row_of(z, x, place, tok_count)
        row = jnp.where(place < 0, -1, row)
        rows = jnp.arange(all_rows, dtype=jnp.int32)
        pick = (row[:, None] == rows[None, :]).astype(BF)
        block = all_rows // (NY * NC)
        device = rows // block
        device = (device // NC + lax.axis_index("y")) % NY * NC + (device + lax.axis_index("c")) % NC
        held_row = device * block + rows % block
        put = (held_row[:, None] == row[None, :]).astype(BF)

    with jax.named_scope("low_rank"):
        incoming_rows = jnp.dot(pick, shard_rows, preferred_element_type=F32)
        incoming_rows = incoming_rows.astype(BF)
        incoming_rows = incoming_rows.reshape(resident, peers * most, width)
        low = jnp.einsum(
            "csk,cko->cso", incoming_rows, adapter_down_weight, preferred_element_type=F32
        ).astype(BF)
        back = jnp.einsum(
            "csf,cxf->csx", incoming_gradients, adapter_up_weight, preferred_element_type=F32
        ).astype(BF)
    with jax.named_scope("sum_low_rank"):
        both = sum_over_tensor(jnp.concatenate([low, back], 0))
        low, back = both[:resident], both[resident:]
    with jax.named_scope("adapter_out"):
        expert_out = jnp.einsum(
            "csx,cxo->cso", low, adapter_up_weight, preferred_element_type=F32
        ).astype(BF)
        expert_out = expert_out.reshape(slots, width)
        weighted = (weight[:, None] * expert_out.astype(F32)).astype(BF)
    with jax.named_scope("adapter_grads"):
        grad_up = jnp.einsum(
            "csr,csd->crd", low, incoming_gradients, preferred_element_type=F32
        ).astype(BF)
        grad_down = jnp.einsum(
            "csd,csr->cdr", incoming_rows, back, preferred_element_type=F32
        ).astype(BF)

    with jax.named_scope("gather_hidden"):
        pieces = gather_hidden(hidden)
    with jax.named_scope("down"):
        down_weight = jnp.concatenate([frozen_down_weight, weighted], 0)
        put = put.reshape(NY, -1, slots)
        out = [
            jnp.dot(
                jnp.concatenate([piece, put[d]], 1), down_weight, preferred_element_type=F32
            ).astype(BF)
            for d, piece in enumerate(pieces)
        ]
        out = jnp.concatenate(out, 0)
        out, grad_up, grad_down = lax.optimization_barrier((out, grad_up, grad_down))
    with jax.named_scope("reduce_rows"):
        ffn_out = reduce_rows(in_order(out)).astype(BF)
    return (ffn_out, grad_down, grad_up)


def solution(mesh):
    split = Mesh(mesh.devices.reshape(NZ, NX, NY, NC), ("z", "x", "y", "c"))
    e, t = ("z", "x"), ("y", "c")
    placed = (
        P(e, t),
        P(t, e),
        P(t, e),
        P(e, t),
        P(e, t, None),
        P(e, None, t),
        P(e, None),
        P(e, None),
        P(e, t),
    )
    return jax.shard_map(
        per_device,
        mesh=split,
        in_specs=placed,
        out_specs=(P(e, t), P(e, t, None), P(e, None, t)),
        check_vma=False,
    )
```
